768 devices in a mesh: rep: 48 (over x, z_lo, core), fsdp: 16 (over y, z_hi).
Axes of the slice: x: 4, y: 8, z: 12 (z_hi: 2, z_lo: 6; z = z_hi * 6 + z_lo), core: 2. Of those that a mesh axis runs over, the one named last changes fastest.
Arguments:
- attn_heads: bfloat16 [196608, 2560], P(('rep', 'fsdp')), may hold values from -6 to 6
- proj_weight: bfloat16 [48, 2560, 2560], P('rep', 'fsdp'), may hold values from -0.125 to 0.125
- base_frag: bfloat16 [768, 5120], P('fsdp'), may hold values from -6 to 6
- local_frag: bfloat16 [48, 768, 5120], P('rep', 'fsdp'), may hold values from -6 to 6
- block_exps: int32 [48, 768, 40], P('rep', 'fsdp'), may hold values from -2 to 2
- momentum: float32 [768, 5120], P('fsdp'), may hold values from -6 to 6
Outputs:
- mixed: bfloat16 [196608, 2560], P(('rep', 'fsdp'))
- new_base: bfloat16 [768, 5120], P('fsdp')
- new_momentum: float32 [768, 5120], P('fsdp')
The draws below stay inside these ranges and needn't reach their ends.
All inputs are finite; a program needn't handle non-finite values.
Results may differ from the reference program's by a relative error of at most 0.0028.
Values may be sent and summed in bfloat16 or wider, within the bound.
No kernel may reach another device: no remote copies, remote signals or barrier semaphores. Data moves between devices by JAX's collectives and lax.ppermute only.
A program may use at most 64 MiB of HBM per device.

```python
import jax
import jax.numpy as jnp
from jax import lax

HW = 2560
DO = 2560
D = 5120
TOKENS = 196608
FRAG_ROWS = 768
N_REP = 48


def with_ends(array, rng, low, top_value):
    dims = array.shape
    index_at = [jax.random.randint(jax.random.fold_in(rng, axis), (), 0, dims[axis]) for axis in range(len(dims))]
    array = array.at[tuple(index_at)].set(low)
    longest = dims.index(max(dims))
    index_at[longest] = (index_at[longest] + 1) % dims[longest]
    return array.at[tuple(index_at)].set(top_value)


def levels(stream_key, extent, cuts, smallest, largest):
    loudness, own = 1.0, jax.random.fold_in(stream_key, 6)
    for position, blocks in cuts:
        draws = jnp.exp(jax.random.uniform(jax.random.fold_in(own, position), (blocks,), jnp.float32, smallest / len(cuts), largest / len(cuts)))
        loudness = loudness * jnp.repeat(draws, extent[position] // blocks).reshape([-1 if axis == position else 1 for axis in range(len(extent))])
    return loudness


def noise(stream_key, extent, spread, limit, split=(), dtype=jnp.bfloat16):
    result = jax.random.normal(stream_key, extent, jnp.float32) * spread
    if len(split) > 0:
        result = levels(stream_key, extent, split, -0.22, 0.18) * result
    return jnp.clip(result, min=-limit, max=limit).astype(dtype)


def setup_inputs(seed: int = 0) -> dict:
    arg_keys = jax.random.split(jax.random.key(seed), 7)
    attn_heads = noise(arg_keys[0], (TOKENS, HW), 1.0, 6.0, ((0, 768),))
    proj_weight = noise(arg_keys[1], (N_REP, HW, DO), HW ** -0.5, 0.125, ((0, 48), (1, 16)))
    base_frag = noise(arg_keys[2], (FRAG_ROWS, D), 1.0, 6.0, ((0, 16),))
    local_frag = noise(arg_keys[3], (N_REP, FRAG_ROWS, D), 1.0, 6.0, ((0, 48), (1, 16)))
    block_exps = with_ends(jax.random.randint(arg_keys[4], (N_REP, FRAG_ROWS, D // 128), -2, 3), jax.random.fold_in(arg_keys[4], 1), -2, 2).astype(jnp.int32)
    momentum = noise(arg_keys[5], (FRAG_ROWS, D), 1.0, 6.0, ((0, 16),), jnp.float32)
    return {"attn_heads": attn_heads, "proj_weight": proj_weight, "base_frag": base_frag, "local_frag": local_frag, "block_exps": block_exps, "momentum": momentum}


def reference(attn_heads, proj_weight, base_frag, local_frag, block_exps, momentum):
    heads = attn_heads.reshape(N_REP, TOKENS // N_REP, HW)

    def project(pair):
        return jnp.dot(pair[0], pair[1], preferred_element_type=jnp.float32).astype(jnp.bfloat16)

    mixed = lax.map(project, (heads, proj_weight)).reshape(TOKENS, DO)
    base_wide = base_frag.astype(jnp.float32)

    def accumulate(total, pair):
        scale = jnp.repeat(jnp.exp2(pair[1].astype(jnp.float32)), 128, axis=1)
        inverse = jnp.repeat(jnp.exp2(-pair[1].astype(jnp.float32)), 128, axis=1)
        level = jnp.clip((base_wide - pair[0].astype(jnp.float32)) * inverse, -1.0, 1.0)
        level = lax.optimization_barrier(level.astype(jnp.bfloat16)).astype(jnp.float32)
        return total + level * scale, None

    total, unused = lax.scan(accumulate, jnp.zeros((FRAG_ROWS, D), jnp.float32), (local_frag, block_exps))
    outer_grad = total / N_REP
    new_momentum = 0.9 * momentum + outer_grad
    new_base = (base_wide - 0.7 * (outer_grad + 0.9 * new_momentum)).astype(jnp.bfloat16)
    return mixed, new_base, new_momentum
```

```python
import jax
import jax.numpy as jnp
from jax import lax
from jax.experimental import pallas as pl
from jax.experimental.pallas import tpu as pltpu
from jax.sharding import PartitionSpec as P

HALF = 80
Y, ZH, ZL, X, C = 8, 2, 6, 4, 2


def moved(to):
    def place(x, y, z, c):
        return (((x * ZL + z % ZL) * C + c) * Y + y) * ZH + z // ZL

    return [
        (place(x, y, z, c), place(*to(x, y, z, c)))
        for x in range(X)
        for y in range(Y)
        for z in range(ZL * ZH)
        for c in range(C)
    ]


UP = moved(lambda x, y, z, c: (x, (y + 1) % Y, z, c))
DOWN = moved(lambda x, y, z, c: (x, (y - 1) % Y, z, c))
AHEAD = moved(lambda x, y, z, c: (x, y, (z + 2) % (ZL * ZH), c))
BACK = moved(lambda x, y, z, c: (x, y, (z - 2) % (ZL * ZH), c))
CORE = moved(lambda x, y, z, c: (x, y, z, 1 - c))
X_FAR = moved(lambda x, y, z, c: (x ^ 2, y, z, c))
X_NEAR = moved(lambda x, y, z, c: (x ^ 1, y, z, c))
Z_PAIR = moved(lambda x, y, z, c: (x, y, z ^ 1, c))
Z_TWO = moved(lambda x, y, z, c: (x, y, (z // ZL) * ZL + (z % ZL + 2) % ZL, c))
Z_FOUR = moved(lambda x, y, z, c: (x, y, (z // ZL) * ZL + (z % ZL + 4) % ZL, c))


def send_to(array, pairs):
    return lax.ppermute(array, ("rep", "fsdp"), pairs)


def product(slots, tokens, picks, weights, total, out_dtype):
    rows, width = tokens.shape[1], weights[0].shape[1]
    tile, count = 512, len(weights)

    def kernel(slots_ref, *refs):
        del slots_ref
        out = refs[-1]
        acc = jnp.zeros((rows, tile), jnp.float32) if total is None else refs[-2][...]
        for block, weight in zip(refs[:count], refs[count : 2 * count]):
            acc += jnp.dot(block[0], weight[...], preferred_element_type=jnp.float32)
        out[...] = acc.astype(out_dtype)

    def block_of(slot):
        return pl.BlockSpec((1,) + tokens.shape[1:], lambda j, at: (at[slot], 0, 0))

    in_specs = [block_of(slot) for slot in picks]
    in_specs += [pl.BlockSpec((w.shape[0], tile), lambda j, at: (0, j)) for w in weights]
    operands = [slots] + [tokens] * count + list(weights)
    if total is not None:
        in_specs.append(pl.BlockSpec((rows, tile), lambda j, at: (0, j)))
        operands.append(total)
    depth = sum(w.shape[0] for w in weights)
    return pl.pallas_call(
        kernel,
        grid_spec=pltpu.PrefetchScalarGridSpec(
            num_scalar_prefetch=1,
            grid=(width // tile,),
            in_specs=in_specs,
            out_specs=pl.BlockSpec((rows, tile), lambda j, at: (0, j)),
        ),
        out_shape=jax.ShapeDtypeStruct((rows, width), out_dtype),
        compiler_params=pltpu.CompilerParams(vmem_limit_bytes=24 << 20),
        cost_estimate=pl.CostEstimate(
            flops=2 * rows * width * depth,
            bytes_accessed=2 * width * depth + 6 * rows * width,
            transcendentals=0,
        ),
    )(*operands)


def fragment_term(base_wide, local_frag, block_exps):
    exps = block_exps.astype(jnp.float32)
    scale = jnp.repeat(jnp.exp2(exps), 128, axis=1)
    inverse = jnp.repeat(jnp.exp2(-exps), 128, axis=1)
    level = jnp.clip((base_wide - local_frag.astype(jnp.float32)) * inverse, -1.0, 1.0)
    return level.astype(jnp.bfloat16) * scale.astype(jnp.bfloat16)


def keep_and_send(array, index, axis):
    half = array.shape[axis] // 2
    first = lax.slice_in_dim(array, 0, half, axis=axis)
    second = lax.slice_in_dim(array, half, 2 * half, axis=axis)
    return jnp.where(index == 0, first, second), jnp.where(index == 0, second, first)


def join(mine, other, index, axis):
    return jnp.concatenate(
        [jnp.where(index == 0, mine, other), jnp.where(index == 0, other, mine)], axis=axis
    )


def together(*arrays):
    return lax.optimization_barrier(arrays)


def per_device(attn_heads, proj_weight, base_frag, local_frag, block_exps, momentum):
    own = proj_weight[0]
    index = lax.axis_index("fsdp")
    y, h = index // ZH, index % ZH
    index = lax.axis_index("rep")
    core, z, x = index % C, (index // C) % ZL, index // (C * ZL)
    far, near, third = x // 2, x % 2, z // 2
    base_wide = base_frag.astype(jnp.float32)

    up1, down1 = send_to(own, UP), send_to(own, DOWN)
    ahead, back = send_to(own[:HALF], AHEAD), send_to(own[HALF:], BACK)
    keep, give = keep_and_send(fragment_term(base_wide, local_frag[0], block_exps[0]), core, 0)
    part = keep.astype(jnp.float32) + send_to(give, CORE).astype(jnp.float32)
    up1, down1, ahead, back, part = together(up1, down1, ahead, back, part)

    up2, down2 = send_to(up1, UP), send_to(down1, DOWN)
    ahead, back = send_to(ahead, AHEAD), send_to(back, BACK)
    keep, give = keep_and_send(part, far, 1)
    part = keep + send_to(give, X_FAR)
    up2, down2, ahead, back, part = together(up2, down2, ahead, back, part)

    up3, down3 = send_to(up2, UP), send_to(down2, DOWN)
    ahead, back = send_to(ahead, AHEAD), send_to(back, BACK)
    keep, give = keep_and_send(part, near, 1)
    part = keep + send_to(give, X_NEAR)
    up3, down3, ahead, back, part, heads = together(up3, down3, ahead, back, part, attn_heads)
    other = jnp.concatenate([ahead, back], axis=0)

    up4, over_down1 = send_to(up3, UP), send_to(other, DOWN)
    part = part + send_to(part, Z_PAIR)
    rows = attn_heads.shape[0]
    tokens = heads.reshape(rows, Y * ZH, 2 * HALF).transpose(1, 0, 2)
    turn = ((y + jnp.arange(Y)) % Y) * ZH
    slots = jnp.concatenate([turn + h, turn + (1 - h)]).astype(jnp.int32)
    up4, over_down1, part, tokens, other = together(up4, over_down1, part, tokens, other)

    over_up1, over_down2 = send_to(other, UP), send_to(over_down1, DOWN)
    two, four = send_to(part, Z_TWO), send_to(part, Z_FOUR)
    zero = jnp.where(third == 0, part, jnp.where(third == 1, two, four))
    one = jnp.where(third == 1, part, jnp.where(third == 2, two, four))
    last = jnp.where(third == 2, part, jnp.where(third == 0, two, four))
    part = (zero + one) + last
    total = product(
        slots,
        tokens,
        (0, 7, 1, 6, 2, 5, 3, 4),
        [own, up1, down1, up2, down2, up3, down3, up4],
        None,
        jnp.float32,
    )
    over_up1, over_down2, part, total = together(over_up1, over_down2, part, total)

    over_up2, over_down3 = send_to(over_up1, UP), send_to(over_down2, DOWN)
    part = join(part, send_to(part, X_NEAR), near, 1)
    part = join(part, send_to(part, X_FAR), far, 1)
    over_up2, over_down3, part = together(over_up2, over_down3, part)

    over_up3, over_down4 = send_to(over_up2, UP), send_to(over_down3, DOWN)
    outer_grad = join(part, send_to(part, CORE), core, 0) / (X * ZL * C)
    new_momentum = 0.9 * momentum + outer_grad
    new_base = (base_wide - 0.7 * (outer_grad + 0.9 * new_momentum)).astype(jnp.bfloat16)
    total = product(
        slots,
        tokens,
        (8, 15, 9, 14, 10, 11),
        [other, over_up1, over_down1, over_up2, over_down2, over_down3],
        total,
        jnp.float32,
    )
    over_up3, over_down4, total, new_momentum, new_base = together(
        over_up3, over_down4, total, new_momentum, new_base
    )
    mixed = product(slots, tokens, (13, 12), [over_up3, over_down4], total, jnp.bfloat16)
    return mixed, new_base, new_momentum


def solution(mesh):
    return jax.shard_map(
        per_device,
        mesh=mesh,
        in_specs=(
            P(("rep", "fsdp"), None),
            P("rep", "fsdp", None),
            P("fsdp", None),
            P("rep", "fsdp", None),
            P("rep", "fsdp", None),
            P("fsdp", None),
        ),
        out_specs=(P(("rep", "fsdp"), None), P("fsdp", None), P("fsdp", None)),
        check_vma=False,
    )
```

```python
import jax
import jax.numpy as jnp
from jax import lax
from jax.experimental import pallas as pl
from jax.experimental.pallas import tpu as pltpu
from jax.sharding import PartitionSpec as P

Y, ZH, ZL, X, C = 8, 2, 6, 4, 2


def moved(to):
    def place(x, y, z, c):
        return (((x * ZL + z % ZL) * C + c) * Y + y) * ZH + z // ZL

    return [
        (place(x, y, z, c), place(*to(x, y, z, c)))
        for x in range(X)
        for y in range(Y)
        for z in range(ZL * ZH)
        for c in range(C)
    ]


UP = moved(lambda x, y, z, c: (x, (y + 1) % Y, z, c))
DOWN = moved(lambda x, y, z, c: (x, (y - 1) % Y, z, c))
CROSS = moved(lambda x, y, z, c: (x, y, (z + ZL) % (ZL * ZH), c))
CORE = moved(lambda x, y, z, c: (x, y, z, 1 - c))
X_FAR = moved(lambda x, y, z, c: (x ^ 2, y, z, c))
X_NEAR = moved(lambda x, y, z, c: (x ^ 1, y, z, c))
Z_PAIR = moved(lambda x, y, z, c: (x, y, z ^ 1, c))
Z_TWO = moved(lambda x, y, z, c: (x, y, (z // ZL) * ZL + (z % ZL + 2) % ZL, c))
Z_FOUR = moved(lambda x, y, z, c: (x, y, (z // ZL) * ZL + (z % ZL + 4) % ZL, c))


def send_to(array, pairs):
    return lax.ppermute(array, ("rep", "fsdp"), pairs)


def product(slot, tokens, weights, total, out_dtype):
    rows, depth = tokens.shape[1:]
    width = weights.shape[1]
    tile = width // 2

    def kernel(slot_ref, *refs):
        del slot_ref
        acc = jnp.dot(refs[0][0], refs[1][...], preferred_element_type=jnp.float32)
        if total is not None:
            acc += refs[2][...]
        refs[-1][...] = acc.astype(out_dtype)

    in_specs = [
        pl.BlockSpec((1, rows, depth), lambda j, at: (at[0], 0, 0)),
        pl.BlockSpec((depth, tile), lambda j, at: (0, j)),
    ]
    operands = [slot, tokens, weights]
    if total is not None:
        in_specs.append(pl.BlockSpec((rows, tile), lambda j, at: (0, j)))
        operands.append(total)
    return pl.pallas_call(
        kernel,
        grid_spec=pltpu.PrefetchScalarGridSpec(
            num_scalar_prefetch=1,
            grid=(width // tile,),
            in_specs=in_specs,
            out_specs=pl.BlockSpec((rows, tile), lambda j, at: (0, j)),
        ),
        out_shape=jax.ShapeDtypeStruct((rows, width), out_dtype),
        compiler_params=pltpu.CompilerParams(vmem_limit_bytes=56 << 20),
        cost_estimate=pl.CostEstimate(
            flops=2 * rows * width * depth,
            bytes_accessed=2 * width * depth + 6 * rows * width,
            transcendentals=0,
        ),
    )(*operands)


def fragment_term(base_wide, local_frag, block_exps):
    exps = block_exps.astype(jnp.float32)
    scale = jnp.repeat(jnp.exp2(exps), 128, axis=1)
    inverse = jnp.repeat(jnp.exp2(-exps), 128, axis=1)
    level = jnp.clip((base_wide - local_frag.astype(jnp.float32)) * inverse, -1.0, 1.0)
    return level.astype(jnp.bfloat16) * scale.astype(jnp.bfloat16)


def keep_and_send(array, index, axis):
    half = array.shape[axis] // 2
    first = lax.slice_in_dim(array, 0, half, axis=axis)
    second = lax.slice_in_dim(array, half, 2 * half, axis=axis)
    return jnp.where(index == 0, first, second), jnp.where(index == 0, second, first)


def join(mine, other, index, axis):
    return jnp.concatenate(
        [jnp.where(index == 0, mine, other), jnp.where(index == 0, other, mine)], axis=axis
    )


def together(*arrays):
    return lax.optimization_barrier(arrays)


def gather_y(array):
    groups = [[y * ZH + h for y in range(Y)] for h in range(ZH)]
    return lax.all_gather(array, "fsdp", axis=0, tiled=True, axis_index_groups=groups)


def per_device(attn_heads, proj_weight, base_frag, local_frag, block_exps, momentum):
    own = proj_weight[0]
    h = lax.axis_index("fsdp") % ZH
    index = lax.axis_index("rep")
    core, z, x = index % C, (index // C) % ZL, index // (C * ZL)
    far, near, third = x // 2, x % 2, z // 2
    base_wide = base_frag.astype(jnp.float32)

    gathered = gather_y(own)
    other = send_to(own, CROSS)
    keep, give = keep_and_send(fragment_term(base_wide, local_frag[0], block_exps[0]), core, 0)
    part = keep.astype(jnp.float32) + send_to(give, CORE).astype(jnp.float32)
    keep, give = keep_and_send(part, far, 1)
    part = keep + send_to(give, X_FAR)
    rows, width = attn_heads.shape
    tokens = attn_heads.reshape(rows, Y, ZH, width // (Y * ZH)).transpose(2, 0, 1, 3)
    tokens = tokens.reshape(ZH, rows, width // ZH)
    other, part, tokens = together(other, part, tokens)

    over_gathered = gather_y(other)
    keep, give = keep_and_send(part, near, 1)
    part = keep + send_to(give, X_NEAR)
    total = product(h[None].astype(jnp.int32), tokens, gathered, None, jnp.float32)
    part = part + send_to(part, Z_PAIR)
    part, total = together(part, total)
    two, four = send_to(part, Z_TWO), send_to(part, Z_FOUR)
    zero = jnp.where(third == 0, part, jnp.where(third == 1, two, four))
    one = jnp.where(third == 1, part, jnp.where(third == 2, two, four))
    last = jnp.where(third == 2, part, jnp.where(third == 0, two, four))
    part = (zero + one) + last
    part = join(part, send_to(part, X_NEAR), near, 1)
    part = join(part, send_to(part, X_FAR), far, 1)
    outer_grad = join(part, send_to(part, CORE), core, 0) / (X * ZL * C)
    new_momentum = 0.9 * momentum + outer_grad
    new_base = (base_wide - 0.7 * (outer_grad + 0.9 * new_momentum)).astype(jnp.bfloat16)

    total, new_momentum, new_base = together(total, new_momentum, new_base)
    mixed = product((1 - h)[None].astype(jnp.int32), tokens, over_gathered, total, jnp.bfloat16)
    return mixed, new_base, new_momentum


def solution(mesh):
    return jax.shard_map(
        per_device,
        mesh=mesh,
        in_specs=(
            P(("rep", "fsdp"), None),
            P("rep", "fsdp", None),
            P("fsdp", None),
            P("rep", "fsdp", None),
            P("rep", "fsdp", None),
            P("fsdp", None),
        ),
        out_specs=(P(("rep", "fsdp"), None), P("fsdp", None), P("fsdp", None)),
        check_vma=False,
    )
```

```python
import jax
import jax.numpy as jnp
from jax import lax
from jax.experimental import pallas as pl
from jax.experimental.pallas import tpu as pltpu
from jax.sharding import PartitionSpec as P

Y, ZH, ZL, X, C = 8, 2, 6, 4, 2
RING = 48


def moved(to):
    def place(x, y, z, c):
        return (((x * ZL + z % ZL) * C + c) * Y + y) * ZH + z // ZL

    return [
        (place(x, y, z, c), place(*to(x, y, z, c)))
        for x in range(X)
        for y in range(Y)
        for z in range(ZL * ZH)
        for c in range(C)
    ]


UP = moved(lambda x, y, z, c: (x, (y + 1) % Y, z, c))
DOWN = moved(lambda x, y, z, c: (x, (y - 1) % Y, z, c))
CROSS = moved(lambda x, y, z, c: (x, y, (z + ZL) % (ZL * ZH), c))
CORE = moved(lambda x, y, z, c: (x, y, z, 1 - c))
X_FAR = moved(lambda x, y, z, c: (x ^ 2, y, z, c))
X_NEAR = moved(lambda x, y, z, c: (x ^ 1, y, z, c))
Z_PAIR = moved(lambda x, y, z, c: (x, y, z ^ 1, c))
Z_TWO = moved(lambda x, y, z, c: (x, y, (z // ZL) * ZL + (z % ZL + 2) % ZL, c))
Z_FOUR = moved(lambda x, y, z, c: (x, y, (z // ZL) * ZL + (z % ZL + 4) % ZL, c))


def send_to(array, pairs):
    return lax.ppermute(array, ("rep", "fsdp"), pairs)


def product(slot, pairs, total, out_dtype):
    rows, width = pairs[0][0].shape[1], pairs[0][1].shape[1]
    tile = width // 2

    def kernel(slot_ref, *refs):
        del slot_ref
        acc = None if total is None else refs[-2][...]
        for i in range(len(pairs)):
            left, right = refs[2 * i][0], refs[2 * i + 1][...]
            term = jnp.dot(left, right, preferred_element_type=jnp.float32)
            acc = term if acc is None else acc + term
        refs[-1][...] = acc.astype(out_dtype)

    in_specs, operands, depth = [], [slot], 0
    for tokens, weights in pairs:
        if tokens.shape[0] == ZH:
            in_specs.append(pl.BlockSpec((1,) + tokens.shape[1:], lambda j, at: (at[0], 0, 0)))
        else:
            in_specs.append(pl.BlockSpec((1,) + tokens.shape[1:], lambda j, at: (0, 0, 0)))
        in_specs.append(pl.BlockSpec((weights.shape[0], tile), lambda j, at: (0, j)))
        operands += [tokens, weights]
        depth += weights.shape[0]
    if total is not None:
        in_specs.append(pl.BlockSpec((rows, tile), lambda j, at: (0, j)))
        operands.append(total)
    return pl.pallas_call(
        kernel,
        grid_spec=pltpu.PrefetchScalarGridSpec(
            num_scalar_prefetch=1,
            grid=(width // tile,),
            in_specs=in_specs,
            out_specs=pl.BlockSpec((rows, tile), lambda j, at: (0, j)),
        ),
        out_shape=jax.ShapeDtypeStruct((rows, width), out_dtype),
        compiler_params=pltpu.CompilerParams(vmem_limit_bytes=56 << 20),
        cost_estimate=pl.CostEstimate(
            flops=2 * rows * width * depth,
            bytes_accessed=2 * width * depth + 6 * rows * width,
            transcendentals=0,
        ),
    )(*operands)


def fragment_term(base_frag, local_frag, block_exps):
    def kernel(base, local, exps, out):
        power = exps[...].astype(jnp.float32)
        scale = jnp.exp2(power).astype(jnp.bfloat16).astype(jnp.float32)
        inverse = jnp.exp2(-power).astype(jnp.bfloat16).astype(jnp.float32)
        for block in range(exps.shape[1]):
            at = pl.ds(block * 128, 128)
            gap = base[:, at].astype(jnp.float32) - local[:, at].astype(jnp.float32)
            level = jnp.clip(gap * inverse[:, block : block + 1], -1.0, 1.0)
            level = level.astype(jnp.bfloat16).astype(jnp.float32)
            out[:, at] = (level * scale[:, block : block + 1]).astype(jnp.bfloat16)

    return pl.pallas_call(
        kernel,
        in_specs=[pl.BlockSpec(memory_space=pltpu.VMEM)] * 3,
        out_specs=pl.BlockSpec(memory_space=pltpu.VMEM),
        out_shape=jax.ShapeDtypeStruct(base_frag.shape, jnp.bfloat16),
        cost_estimate=pl.CostEstimate(flops=0, bytes_accessed=4 << 20, transcendentals=0),
    )(base_frag, local_frag, block_exps)


def keep_and_send(array, index, axis):
    half = array.shape[axis] // 2
    first = lax.slice_in_dim(array, 0, half, axis=axis)
    second = lax.slice_in_dim(array, half, 2 * half, axis=axis)
    return jnp.where(index == 0, first, second), jnp.where(index == 0, second, first)


def join(mine, other, index, axis):
    return jnp.concatenate(
        [jnp.where(index == 0, mine, other), jnp.where(index == 0, other, mine)], axis=axis
    )


def together(*arrays):
    return lax.optimization_barrier(arrays)


def gather_y(array):
    groups = [[y * ZH + h for y in range(Y)] for h in range(ZH)]
    return lax.all_gather(array, "fsdp", axis=0, tiled=True, axis_index_groups=groups)


def per_device(attn_heads, proj_weight, base_frag, local_frag, block_exps, momentum):
    own = proj_weight[0]
    index = lax.axis_index("fsdp")
    y, h = index // ZH, index % ZH
    index = lax.axis_index("rep")
    core, z, x = index % C, (index // C) % ZL, index // (C * ZL)
    far, near, third = x // 2, x % 2, z // 2
    base_wide = base_frag.astype(jnp.float32)

    depth = own.shape[0]
    whole = depth - RING
    gathered = gather_y(own[:whole])
    other = send_to(own, CROSS)
    term = fragment_term(base_frag, local_frag[0], block_exps[0])
    term, mine = together(term, own[whole:])
    up1, down1 = send_to(mine, UP), send_to(mine, DOWN)
    up2, down2 = send_to(up1, UP), send_to(down1, DOWN)
    keep, give = keep_and_send(term, core, 0)
    part = keep.astype(jnp.float32) + send_to(give, CORE).astype(jnp.float32)
    keep, give = keep_and_send(part, far, 1)
    part = keep + send_to(give, X_FAR)
    rows, width = attn_heads.shape
    shards = attn_heads.reshape(rows, Y, ZH, depth).transpose(2, 0, 1, 3)
    tokens = shards.reshape(ZH, rows, width // ZH)
    near_tokens = shards[..., :whole].reshape(ZH, rows, Y * whole)
    turned = jnp.where(h == 0, shards[0], shards[1])[..., whole:]
    turned = lax.dynamic_slice_in_dim(jnp.concatenate([turned, turned], axis=1), y, Y, 1)
    turned = turned.reshape(1, rows, Y * RING)
    other, part, tokens, near_tokens, turned, up2, down2 = together(
        other, part, tokens, near_tokens, turned, up2, down2
    )

    over_gathered = gather_y(other)
    up3, down3 = send_to(up2, UP), send_to(down2, DOWN)
    up4 = send_to(up3, UP)
    ringed = jnp.concatenate([mine, down1, down2, down3, up4, up3, up2, up1], axis=0)
    keep, give = keep_and_send(part, near, 1)
    part = keep + send_to(give, X_NEAR)
    pairs = [(near_tokens, gathered), (turned, ringed)]
    total = product(h[None].astype(jnp.int32), pairs, None, jnp.float32)
    part = part + send_to(part, Z_PAIR)
    two, four = send_to(part, Z_TWO), send_to(part, Z_FOUR)
    zero = jnp.where(third == 0, part, jnp.where(third == 1, two, four))
    one = jnp.where(third == 1, part, jnp.where(third == 2, two, four))
    last = jnp.where(third == 2, part, jnp.where(third == 0, two, four))
    part = (zero + one) + last
    part = join(part, send_to(part, X_NEAR), near, 1)
    part = join(part, send_to(part, X_FAR), far, 1)
    outer_grad = join(part, send_to(part, CORE), core, 0) / (X * ZL * C)
    new_momentum = 0.9 * momentum + outer_grad
    new_base = (base_wide - 0.7 * (outer_grad + 0.9 * new_momentum)).astype(jnp.bfloat16)

    total, new_momentum, new_base = together(total, new_momentum, new_base)
    pairs = [(tokens, over_gathered)]
    mixed = product((1 - h)[None].astype(jnp.int32), pairs, total, jnp.bfloat16)
    return mixed, new_base, new_momentum


def solution(mesh):
    return jax.shard_map(
        per_device,
        mesh=mesh,
        in_specs=(
            P(("rep", "fsdp"), None),
            P("rep", "fsdp", None),
            P("fsdp", None),
            P("rep", "fsdp", None),
            P("rep", "fsdp", None),
            P("fsdp", None),
        ),
        out_specs=(P(("rep", "fsdp"), None), P("fsdp", None), P("fsdp", None)),
        check_vma=False,
    )
```

```python
import jax
import jax.numpy as jnp
from jax import lax
from jax.experimental import pallas as pl
from jax.experimental.pallas import tpu as pltpu
from jax.sharding import PartitionSpec as P

Y, ZH, ZL, X, C = 8, 2, 6, 4, 2
RING = 48


def moved(to):
    def place(x, y, z, c):
        return (((x * ZL + z % ZL) * C + c) * Y + y) * ZH + z // ZL

    return [
        (place(x, y, z, c), place(*to(x, y, z, c)))
        for x in range(X)
        for y in range(Y)
        for z in range(ZL * ZH)
        for c in range(C)
    ]


UP = moved(lambda x, y, z, c: (x, (y + 1) % Y, z, c))
DOWN = moved(lambda x, y, z, c: (x, (y - 1) % Y, z, c))
CROSS = moved(lambda x, y, z, c: (x, y, (z + ZL) % (ZL * ZH), c))
CORE = moved(lambda x, y, z, c: (x, y, z, 1 - c))
X_FAR = moved(lambda x, y, z, c: (x ^ 2, y, z, c))
X_NEAR = moved(lambda x, y, z, c: (x ^ 1, y, z, c))
Z_PAIR = moved(lambda x, y, z, c: (x, y, z ^ 1, c))
Z_TWO = moved(lambda x, y, z, c: (x, y, (z // ZL) * ZL + (z % ZL + 2) % ZL, c))
Z_FOUR = moved(lambda x, y, z, c: (x, y, (z // ZL) * ZL + (z % ZL + 4) % ZL, c))


def send_to(array, pairs):
    return lax.ppermute(array, ("rep", "fsdp"), pairs)


def product(slot, pairs, total, out_dtype):
    rows, width = pairs[0][0].shape[1], pairs[0][1].shape[1]
    tile = width // 2

    def kernel(slot_ref, *refs):
        del slot_ref
        acc = None if total is None else refs[-2][...]
        for i in range(len(pairs)):
            left, right = refs[2 * i][0], refs[2 * i + 1][...]
            term = jnp.dot(left, right, preferred_element_type=jnp.float32)
            acc = term if acc is None else acc + term
        refs[-1][...] = acc.astype(out_dtype)

    in_specs, operands, depth = [], [slot], 0
    for tokens, weights in pairs:
        if tokens.shape[0] == ZH:
            in_specs.append(pl.BlockSpec((1,) + tokens.shape[1:], lambda j, at: (at[0], 0, 0)))
        else:
            in_specs.append(pl.BlockSpec((1,) + tokens.shape[1:], lambda j, at: (0, 0, 0)))
        in_specs.append(pl.BlockSpec((weights.shape[0], tile), lambda j, at: (0, j)))
        operands += [tokens, weights]
        depth += weights.shape[0]
    if total is not None:
        in_specs.append(pl.BlockSpec((rows, tile), lambda j, at: (0, j)))
        operands.append(total)
    return pl.pallas_call(
        kernel,
        grid_spec=pltpu.PrefetchScalarGridSpec(
            num_scalar_prefetch=1,
            grid=(width // tile,),
            in_specs=in_specs,
            out_specs=pl.BlockSpec((rows, tile), lambda j, at: (0, j)),
        ),
        out_shape=jax.ShapeDtypeStruct((rows, width), out_dtype),
        compiler_params=pltpu.CompilerParams(vmem_limit_bytes=56 << 20),
        cost_estimate=pl.CostEstimate(
            flops=2 * rows * width * depth,
            bytes_accessed=2 * width * depth + 6 * rows * width,
            transcendentals=0,
        ),
    )(*operands)


def fragment_term(base_wide, local_frag, block_exps):
    exps = block_exps.astype(jnp.float32)
    scale = jnp.repeat(jnp.exp2(exps), 128, axis=1)
    inverse = jnp.repeat(jnp.exp2(-exps), 128, axis=1)
    level = jnp.clip((base_wide - local_frag.astype(jnp.float32)) * inverse, -1.0, 1.0)
    return level.astype(jnp.bfloat16) * scale.astype(jnp.bfloat16)


def keep_and_send(array, index, axis):
    half = array.shape[axis] // 2
    first = lax.slice_in_dim(array, 0, half, axis=axis)
    second = lax.slice_in_dim(array, half, 2 * half, axis=axis)
    return jnp.where(index == 0, first, second), jnp.where(index == 0, second, first)


def join(mine, other, index, axis):
    return jnp.concatenate(
        [jnp.where(index == 0, mine, other), jnp.where(index == 0, other, mine)], axis=axis
    )


def together(*arrays):
    return lax.optimization_barrier(arrays)


def gather_y(array):
    groups = [[y * ZH + h for y in range(Y)] for h in range(ZH)]
    return lax.all_gather(array, "fsdp", axis=0, tiled=True, axis_index_groups=groups)


def per_device(attn_heads, proj_weight, base_frag, local_frag, block_exps, momentum):
    own = proj_weight[0]
    index = lax.axis_index("fsdp")
    y, h = index // ZH, index % ZH
    index = lax.axis_index("rep")
    core, z, x = index % C, (index // C) % ZL, index // (C * ZL)
    far, near, third = x // 2, x % 2, z // 2
    base_wide = base_frag.astype(jnp.float32)

    gathered = gather_y(own)
    other = send_to(own, CROSS)
    keep, give = keep_and_send(fragment_term(base_wide, local_frag[0], block_exps[0]), core, 0)
    part = keep.astype(jnp.float32) + send_to(give, CORE).astype(jnp.float32)
    keep, give = keep_and_send(part, far, 1)
    part = keep + send_to(give, X_FAR)
    rows, width = attn_heads.shape
    depth = own.shape[0]
    whole = depth - RING
    shards = attn_heads.reshape(rows, Y, ZH, depth).transpose(2, 0, 1, 3)
    tokens = shards.reshape(ZH, rows, width // ZH)
    over_tokens = shards[..., :whole].reshape(ZH, rows, Y * whole)
    turned = jnp.where(h == 0, shards[1], shards[0])[..., whole:]
    turned = lax.dynamic_slice_in_dim(jnp.concatenate([turned, turned], axis=1), y, Y, 1)
    turned = turned.reshape(1, rows, Y * RING)
    other, part, tokens, over_tokens, turned = together(other, part, tokens, over_tokens, turned)

    over_gathered = gather_y(other[:whole])
    mine = other[whole:]
    up1, down1 = send_to(mine, UP), send_to(mine, DOWN)
    up2, down2 = send_to(up1, UP), send_to(down1, DOWN)
    up3, down3 = send_to(up2, UP), send_to(down2, DOWN)
    up4 = send_to(up3, UP)
    ringed = jnp.concatenate([mine, down1, down2, down3, up4, up3, up2, up1], axis=0)
    keep, give = keep_and_send(part, near, 1)
    part = keep + send_to(give, X_NEAR)
    total = product(h[None].astype(jnp.int32), [(tokens, gathered)], None, jnp.float32)
    part = part + send_to(part, Z_PAIR)
    part, total = together(part, total)
    two, four = send_to(part, Z_TWO), send_to(part, Z_FOUR)
    zero = jnp.where(third == 0, part, jnp.where(third == 1, two, four))
    one = jnp.where(third == 1, part, jnp.where(third == 2, two, four))
    last = jnp.where(third == 2, part, jnp.where(third == 0, two, four))
    part = (zero + one) + last
    part = join(part, send_to(part, X_NEAR), near, 1)
    part = join(part, send_to(part, X_FAR), far, 1)
    outer_grad = join(part, send_to(part, CORE), core, 0) / (X * ZL * C)
    new_momentum = 0.9 * momentum + outer_grad
    new_base = (base_wide - 0.7 * (outer_grad + 0.9 * new_momentum)).astype(jnp.bfloat16)

    total, ringed, new_momentum, new_base = together(total, ringed, new_momentum, new_base)
    pairs = [(over_tokens, over_gathered), (turned, ringed)]
    mixed = product((1 - h)[None].astype(jnp.int32), pairs, total, jnp.bfloat16)
    return mixed, new_base, new_momentum


def solution(mesh):
    return jax.shard_map(
        per_device,
        mesh=mesh,
        in_specs=(
            P(("rep", "fsdp"), None),
            P("rep", "fsdp", None),
            P("fsdp", None),
            P("rep", "fsdp", None),
            P("rep", "fsdp", None),
            P("fsdp", None),
        ),
        out_specs=(P(("rep", "fsdp"), None), P("fsdp", None), P("fsdp", None)),
        check_vma=False,
    )
```
